128 devices in a mesh: dp: 4 (over x_lo, core), fsdp: 32 (over z, y, x_hi).
Axes of the slice: x: 4 (x_hi: 2, x_lo: 2; x = x_hi * 2 + x_lo), y: 4, z: 4, core: 2. Of those that a mesh axis runs over, the one named last changes fastest.
Arguments:
- partials: bfloat16 [4, 256, 512, 512], P('dp', None, 'fsdp'), may hold values from -2 to 2
- stats_left: float32 [256, 512, 512], P(('dp', 'fsdp')), as said below
- stats_right: float32 [256, 512, 512], P(('dp', 'fsdp')), as said below
- root_left: bfloat16 [256, 512, 512], P(('dp', 'fsdp')), as said below
- root_right: bfloat16 [256, 512, 512], P(('dp', 'fsdp')), as said below
- moment: float32 [256, 512, 512], P(('dp', 'fsdp')), may hold values from -3 to 3
- second: float32 [256, 512, 512], P(('dp', 'fsdp')), may hold values from 0.02 to 1
Outputs:
- stats_left_out: float32 [256, 512, 512], P(('dp', 'fsdp'))
- stats_right_out: float32 [256, 512, 512], P(('dp', 'fsdp'))
- moment_out: float32 [256, 512, 512], P(('dp', 'fsdp'))
- second_out: float32 [256, 512, 512], P(('dp', 'fsdp'))
- step_out: float32 [256, 512, 512], P('dp', 'fsdp')
The draws below stay inside these ranges and needn't reach their ends.
Inputs may be any that keep to these rules, and one draw needn't show every extreme that they name: `stats_left`: each block is symmetric. `stats_right`: each block is symmetric. `root_left`: each block is symmetric. `root_right`: each block is symmetric.
All inputs are finite; a program needn't handle non-finite values.
Results may differ from the reference program's by a relative error of at most 0.0041.
Values may be sent and summed in bfloat16 or wider, within the bound.
No kernel may reach another device: no remote copies, remote signals or barrier semaphores. Data moves between devices by JAX's collectives and lax.ppermute only.
A program may use at most 128 MiB of HBM per device.

```python
import math
import jax
import jax.numpy as jnp
from jax import lax

BS = 512
NBLK = 256
N_DP = 4


def assemble(diag_values, noise, off_scale):
    symmetric = (noise + jnp.swapaxes(noise, 1, 2)) * (off_scale / math.sqrt(2.0))
    identity = jnp.eye(BS, dtype=jnp.float32)
    return symmetric * (1.0 - identity) + diag_values[:, :, None] * identity


def statistic_blocks(key):
    first, later = jax.random.split(key)
    off_scale = 0.25 * math.sqrt(BS)
    noise = jax.random.truncated_normal(first, -3.0, 3.0, (NBLK, BS, BS), jnp.float32)
    diag_values = jnp.exp(jax.random.uniform(later, (NBLK, BS), jnp.float32, math.log(0.05 * BS), math.log(0.5 * BS)))
    return assemble(diag_values, noise, off_scale)


def root_blocks(key):
    first, later = jax.random.split(key)
    off_scale = 0.5 / math.sqrt(BS)
    noise = jax.random.truncated_normal(first, -3.0, 3.0, (NBLK, BS, BS), jnp.float32)
    diag_values = jnp.exp(jax.random.uniform(later, (NBLK, BS), jnp.float32, math.log(0.3), math.log(3.0)))
    return assemble(diag_values, noise, off_scale).astype(jnp.bfloat16)


def draw_stats_left(key, part):
    key = jax.random.fold_in(key, 11)
    return statistic_blocks(key)


def draw_stats_right(key, part):
    key = jax.random.fold_in(key, 23)
    return statistic_blocks(key)


def draw_root_left(key, part):
    key = jax.random.fold_in(key, 37)
    return root_blocks(key)


def draw_root_right(key, part):
    key = jax.random.fold_in(key, 41)
    return root_blocks(key)


def strengthened(drawn, stream_key, source, target, parts, factor):
    owner, partner = [(jnp.arange(drawn.shape[axis_at]) // (drawn.shape[axis_at] // parts)).reshape([-1 if axis == axis_at else 1 for axis in range(drawn.ndim)]) for axis_at in (source, target)]
    chosen = jax.random.permutation(stream_key, parts)[partner]
    strong = (owner == chosen) | (owner == (partner + parts // 2) % parts)
    return jnp.where(strong, factor * drawn, drawn)


def shard_levels(stream_key, extent, cuts, smallest, high):
    level = 1.0
    for position, shards_of in cuts:
        steps = jax.random.uniform(jax.random.fold_in(jax.random.fold_in(stream_key, 6), position), (shards_of,), jnp.float32, smallest / len(cuts), high / len(cuts))
        level = level * jnp.repeat(jnp.exp(steps), extent[position] // shards_of).reshape((-1,) + (1,) * (len(extent) - 1 - position))
    return level


def bell_draw(key, extent, width, limit, pieces=(), kind=jnp.bfloat16):
    factor_of = shard_levels(key, extent, pieces, -0.22, 0.18) if pieces else 1.0
    drawn = jax.random.normal(key, extent, jnp.float32) * width * factor_of
    return jnp.minimum(jnp.maximum(drawn, -limit), limit).astype(kind)


def bell_draw_with(key, shape, scale, reach, cuts, heavy, kind=jnp.bfloat16):
    entries = scale * jax.random.normal(key, shape, jnp.float32)
    if cuts:
        entries = entries * shard_levels(key, shape, cuts, -0.22, 0.18)
    return jnp.clip(strengthened(entries, jax.random.fold_in(key, 3), *heavy), -reach, reach).astype(kind)


def setup_inputs(seed: int = 0) -> dict:
    key_of = jax.random.split(jax.random.key(seed), 8)
    return {
        "partials": bell_draw_with(key_of[0], (N_DP, NBLK, BS, BS), 0.25, 2.0, ((0, 4), (2, 32)), (0, 1, 4, 2.0)),
        "stats_left": draw_stats_left(jax.random.fold_in(key_of[7], 71), 0),
        "stats_right": draw_stats_right(jax.random.fold_in(key_of[7], 71), 0),
        "root_left": draw_root_left(jax.random.fold_in(key_of[7], 71), 0),
        "root_right": draw_root_right(jax.random.fold_in(key_of[7], 71), 0),
        "moment": bell_draw(key_of[5], (NBLK, BS, BS), 0.5, 3.0, ((0, 128),), jnp.float32),
        "second": jnp.clip(jnp.exp(math.log(1.0) - 3.912023 * jax.random.uniform(key_of[6], (NBLK, BS, BS), jnp.float32) ** shard_levels(key_of[6], (NBLK, BS, BS), ((0, 128),), -0.2, 0.2)), 0.02, 1.0),
    }


stat_decay = 0.95
moment_decay = 0.9
square_decay = 0.95
adam_epsilon = 1e-08
norm_epsilon = 1e-06

def update_block(inputs):
    gradient, left_stat, right_stat, left_root, right_root, moment_block, second_block = inputs
    highest = lax.Precision.HIGHEST
    gram_left = lax.dot_general(gradient, gradient, (((1,), (1,)), ((), ())), precision=highest, preferred_element_type=jnp.float32)
    gram_right = lax.dot_general(gradient, gradient, (((0,), (0,)), ((), ())), precision=highest, preferred_element_type=jnp.float32)
    left_new = stat_decay * left_stat + (1.0 - stat_decay) * gram_left
    right_new = stat_decay * right_stat + (1.0 - stat_decay) * gram_right
    moment_new = moment_decay * moment_block + (1.0 - moment_decay) * gradient
    second_new = square_decay * second_block + (1.0 - square_decay) * gradient * gradient
    adam_dir = moment_new / (jnp.sqrt(second_new) + adam_epsilon)
    grad_half = gradient.astype(jnp.bfloat16)
    left_applied = jnp.dot(left_root, grad_half, preferred_element_type=jnp.float32).astype(jnp.bfloat16)
    conditioned = jnp.dot(left_applied, right_root, preferred_element_type=jnp.float32)
    graft = jnp.sqrt(jnp.sum(adam_dir * adam_dir)) / (jnp.sqrt(jnp.sum(conditioned * conditioned)) + norm_epsilon)
    return (left_new, right_new, moment_new, second_new, graft * conditioned)

def reference(partials, stats_left, stats_right, root_left, root_right, moment, second):
    gradient = partials[0].astype(jnp.float32)
    for replica in range(1, partials.shape[0]):
        gradient = gradient + partials[replica].astype(jnp.float32)
    left_new, right_new, moment_new, second_new, step_dir = lax.map(update_block, (gradient, stats_left, stats_right, root_left, root_right, moment, second))
    return (left_new, right_new, moment_new, second_new, step_dir)
```

```python
import functools

import jax
import jax.numpy as jnp
from jax import lax
from jax.experimental import pallas as pl
from jax.experimental.pallas import tpu as pltpu
from jax.sharding import Mesh, PartitionSpec as P

stat_decay = 0.95
moment_decay = 0.9
square_decay = 0.95
adam_epsilon = 1e-08
norm_epsilon = 1e-06


def split_half(values):
    high = values.astype(jnp.bfloat16)
    low = (values - high.astype(jnp.float32)).astype(jnp.bfloat16)
    return high, low


def dot(a, b):
    return jnp.dot(a, b, preferred_element_type=jnp.float32)


def pick_kernel(halves, outgoing, sem):
    core = lax.axis_index("core")
    copies = [
        pltpu.make_async_copy(halves.at[n, 1 - core], outgoing.at[n], sem.at[n])
        for n in range(halves.shape[0])
    ]
    for copy in copies:
        copy.start()
    for copy in copies:
        copy.wait()


def pick(halves):
    near, _, *rest = halves.shape
    return pl.pallas_call(
        pick_kernel,
        out_shape=jax.ShapeDtypeStruct((near, *rest), halves.dtype),
        in_specs=[pl.BlockSpec(memory_space=pl.ANY)],
        out_specs=pl.BlockSpec(memory_space=pl.ANY),
        scratch_shapes=[pltpu.SemaphoreType.DMA((near,))],
        compiler_params=pltpu.CompilerParams(vmem_limit_bytes=4 * 2**20),
        name="pick",
    )(pltpu.with_memory_space_constraint(halves, pltpu.HBM))


def preload_kernel(halves, *refs):
    count = (len(refs) - 1) // 2
    sources, targets, sem = refs[:count], refs[count : 2 * count + 1], refs[-1]
    core = lax.axis_index("core")
    near = halves.shape[0]
    copies = [
        pltpu.make_async_copy(halves.at[n, core], targets[0].at[n], sem.at[n]) for n in range(near)
    ]
    for n, (source, target) in enumerate(zip(sources, targets[1:])):
        copies.append(pltpu.make_async_copy(source, target, sem.at[near + n]))
    for copy in copies:
        copy.start()
    for copy in copies:
        copy.wait()


def preload(halves, *arrays):
    near, _, *rest = halves.shape
    size = sum(a.size * a.dtype.itemsize for a in (halves, *arrays))
    return pl.pallas_call(
        preload_kernel,
        out_shape=[pltpu.VMEM((near, *rest), halves.dtype)]
        + [pltpu.VMEM(a.shape, a.dtype) for a in arrays],
        in_specs=[pl.BlockSpec(memory_space=pl.ANY)] * (1 + len(arrays)),
        out_specs=[pl.BlockSpec(memory_space=pl.ANY)] * (1 + len(arrays)),
        scratch_shapes=[pltpu.SemaphoreType.DMA((near + len(arrays),))],
        compiler_params=pltpu.CompilerParams(vmem_limit_bytes=4 * 2**20),
        cost_estimate=pl.CostEstimate(flops=0, bytes_accessed=size, transcendentals=0),
        name="preload",
    )(*(pltpu.with_memory_space_constraint(a, pltpu.HBM) for a in (halves, *arrays)))


def pair_add_kernel(kept, swapped, total):
    rows = 8
    for n in range(kept.shape[0]):
        @pl.loop(0, kept.shape[1], step=rows)
        def _(i):
            at = (n, pl.ds(i, rows))
            total[at] = (kept[at].astype(jnp.float32) + swapped[at].astype(jnp.float32)).astype(total.dtype)


def pair_add(kept, swapped):
    return pl.pallas_call(
        pair_add_kernel,
        out_shape=pltpu.VMEM(kept.shape, kept.dtype),
        in_specs=[pl.BlockSpec(memory_space=pltpu.VMEM)] * 2,
        out_specs=pl.BlockSpec(memory_space=pltpu.VMEM),
        compiler_params=pltpu.CompilerParams(vmem_limit_bytes=8 * 2**20),
        name="pair_add",
    )(kept, pltpu.with_memory_space_constraint(swapped, pltpu.VMEM))


def direction_kernel(arrived, root_left, root_right, moment, second, step, held, sem):
    owned, size = root_left.shape[:2]
    copies = []
    for j in range(owned):
        first = arrived[0, :, j].reshape(size, size).astype(jnp.float32)
        other = arrived[1, :, j].reshape(size, size).astype(jnp.float32)
        gradient = first + other
        moment_new = moment_decay * moment[j] + (1.0 - moment_decay) * gradient
        second_new = square_decay * second[j] + (1.0 - square_decay) * gradient * gradient
        adam_dir = moment_new / (jnp.sqrt(second_new) + adam_epsilon)
        adam_sum = jnp.sum(adam_dir * adam_dir)
        high, low = split_half(gradient)
        left = root_left[j]
        right = root_right[j]
        left_high, left_low = split_half(dot(left, high) + dot(left, low))
        conditioned = dot(left_high, right) + dot(left_low, right)
        cond_sum = jnp.sum(conditioned * conditioned)
        graft = jnp.sqrt(adam_sum) / (jnp.sqrt(cond_sum) + norm_epsilon)
        held[j] = (conditioned * graft).astype(jnp.bfloat16).reshape(held.shape[1:])
        copy = pltpu.make_async_copy(held.at[j], step.at[:, j], sem.at[j])
        copy.start()
        copies.append(copy)
    for copy in copies:
        copy.wait()


def direction(arrived, root_left, root_right, moment, second):
    near, ranks, owned, share, width = arrived.shape
    held = pltpu.VMEM((owned, ranks, share, width), jnp.bfloat16)
    return pl.pallas_call(
        direction_kernel,
        out_shape=pltpu.HBM((ranks, owned, share, width), jnp.bfloat16),
        in_specs=[pl.BlockSpec(memory_space=pltpu.VMEM)] * 5,
        out_specs=pl.BlockSpec(memory_space=pl.ANY),
        scratch_shapes=[held, pltpu.SemaphoreType.DMA((owned,))],
        compiler_params=pltpu.CompilerParams(vmem_limit_bytes=24 * 2**20),
        cost_estimate=pl.CostEstimate(
            flops=owned * 8 * width**3, bytes_accessed=11 * 2**20, transcendentals=0
        ),
        name="direction",
    )(arrived, root_left, root_right, moment, second)


def gram(high, low, contract):
    def product(a, b):
        return lax.dot_general(
            a, b, (((contract,), (contract,)), ((), ())), preferred_element_type=jnp.float32
        )

    return product(high, high) + product(high, low) + product(low, high)


def statistics_kernel(
    arrived, stats_left, stats_right, moment, second, left_new, right_new, moment_new, second_new
):
    size = stats_left.shape[-1]
    first = arrived[0, :, 0].reshape(size, size).astype(jnp.float32)
    other = arrived[1, :, 0].reshape(size, size).astype(jnp.float32)
    gradient = first + other
    moment_new[0] = moment_decay * moment[0] + (1.0 - moment_decay) * gradient
    second_new[0] = square_decay * second[0] + (1.0 - square_decay) * gradient * gradient
    high, low = split_half(gradient)
    left_new[0] = stat_decay * stats_left[0] + (1.0 - stat_decay) * gram(high, low, 1)
    right_new[0] = stat_decay * stats_right[0] + (1.0 - stat_decay) * gram(high, low, 0)


def statistics(arrived, stats_left, stats_right, moment, second):
    near, ranks, owned, share, width = arrived.shape
    square = pl.BlockSpec((1, width, width), lambda j: (j, 0, 0))
    fixed = [pltpu.with_memory_space_constraint(a, pltpu.HBM) for a in (stats_left, stats_right, moment, second)]
    return pl.pallas_call(
        statistics_kernel,
        grid=(owned,),
        out_shape=[jax.ShapeDtypeStruct(stats_left.shape, jnp.float32)] * 4,
        in_specs=[pl.BlockSpec((near, ranks, 1, share, width), lambda j: (0, 0, j, 0, 0))] + [square] * 4,
        out_specs=[square] * 4,
        compiler_params=pltpu.CompilerParams(vmem_limit_bytes=40 * 2**20),
        cost_estimate=pl.CostEstimate(
            flops=owned * 12 * width**3, bytes_accessed=18 * 2**20, transcendentals=0
        ),
        name="statistics",
    )(arrived, *fixed)


def widen_kernel(narrow, wide):
    wide[...] = narrow[...].astype(jnp.float32)


def widen(narrow):
    rows = 16
    count, share, width = narrow.shape
    spec = pl.BlockSpec((rows, share, width), lambda i: (i, 0, 0))
    return pl.pallas_call(
        widen_kernel,
        grid=(count // rows,),
        out_shape=jax.ShapeDtypeStruct(narrow.shape, jnp.float32),
        in_specs=[spec],
        out_specs=spec,
        compiler_params=pltpu.CompilerParams(vmem_limit_bytes=16 * 2**20),
        name="widen",
    )(narrow)


def per_device(partials, stats_left, stats_right, root_left, root_right, moment, second):
    owned_count = stats_left.shape[0]
    fsdp_count = lax.axis_size("fsdp")
    near_count = lax.axis_size("near")
    pieces = partials[0]
    _, row_share, block_width = pieces.shape
    halves = pieces.reshape(near_count, 2, fsdp_count * owned_count, row_share, block_width)
    swapped = lax.ppermute(pick(halves), "core", [(0, 1), (1, 0)])
    kept, left_here, right_here, moment_here, second_here = preload(
        halves, root_left, root_right, moment, second
    )
    pair_sum = pair_add(kept, swapped)
    grouped = pair_sum.reshape(near_count * fsdp_count, owned_count, row_share, block_width)
    arrived = lax.all_to_all(grouped, ("near", "fsdp"), split_axis=0, concat_axis=0, tiled=True)
    arrived = arrived.reshape(near_count, fsdp_count, owned_count, row_share, block_width)
    step = direction(arrived, left_here, right_here, moment_here, second_here)
    returned = lax.all_to_all(step, "fsdp", split_axis=0, concat_axis=0, tiled=True)
    step_out = widen(returned.reshape(fsdp_count * owned_count, row_share, block_width))
    news = statistics(arrived, stats_left, stats_right, moment, second)
    return (*news, step_out)


def solution(mesh):
    fine = Mesh(mesh.devices.reshape(2, 2, -1), ("near", "core", "fsdp"))
    owned = P(("near", "core", "fsdp"), None, None)
    return jax.shard_map(
        per_device,
        mesh=fine,
        in_specs=(P(("near", "core"), None, "fsdp", None), owned, owned, owned, owned, owned, owned),
        out_specs=(owned, owned, owned, owned, P(("near", "core"), "fsdp", None)),
        check_vma=False,
    )
```

```python
import functools

import jax
import jax.numpy as jnp
from jax import lax
from jax.experimental import pallas as pl
from jax.experimental.pallas import tpu as pltpu
from jax.sharding import Mesh, PartitionSpec as P

stat_decay = 0.95
moment_decay = 0.9
square_decay = 0.95
adam_epsilon = 1e-08
norm_epsilon = 1e-06
every_axis = ("near", "core", "fsdp")


def split_half(values):
    high = values.astype(jnp.bfloat16)
    low = (values - high.astype(jnp.float32)).astype(jnp.bfloat16)
    return high, low


def dot(a, b):
    return jnp.dot(a, b, preferred_element_type=jnp.float32)


def pick_kernel(halves, outgoing, sem):
    core = lax.axis_index("core")
    near, cuts = sem.shape
    count = halves.shape[2] // cuts
    copies = []
    for n in range(near):
        for c in range(cuts):
            at = pl.ds(c * count, count)
            copies.append(
                pltpu.make_async_copy(halves.at[n, 1 - core, at], outgoing.at[n, at], sem.at[n, c])
            )
    for copy in copies:
        copy.start()
    for copy in copies:
        copy.wait()


def pick(halves):
    near, _, *rest = halves.shape
    return pl.pallas_call(
        pick_kernel,
        out_shape=jax.ShapeDtypeStruct((near, *rest), halves.dtype),
        in_specs=[pl.BlockSpec(memory_space=pl.ANY)],
        out_specs=pl.BlockSpec(memory_space=pl.ANY),
        scratch_shapes=[pltpu.SemaphoreType.DMA((near, 4))],
        compiler_params=pltpu.CompilerParams(vmem_limit_bytes=4 * 2**20),
        name="pick",
    )(pltpu.with_memory_space_constraint(halves, pltpu.HBM))


def preload_kernel(halves, *refs):
    count = (len(refs) - 1) // 2
    sources, targets, sem = refs[:count], refs[count : 2 * count + 1], refs[-1]
    core = lax.axis_index("core")
    near = halves.shape[0]
    copies = [
        pltpu.make_async_copy(halves.at[n, core], targets[0].at[n], sem.at[n]) for n in range(near)
    ]
    for n, (source, target) in enumerate(zip(sources, targets[1:])):
        copies.append(pltpu.make_async_copy(source, target, sem.at[near + n]))
    for copy in copies:
        copy.start()
    for copy in copies:
        copy.wait()


def preload(halves, *arrays):
    near, _, *rest = halves.shape
    size = sum(a.size * a.dtype.itemsize for a in (halves, *arrays))
    return pl.pallas_call(
        preload_kernel,
        out_shape=[pltpu.VMEM((near, *rest), halves.dtype)]
        + [pltpu.VMEM(a.shape, a.dtype) for a in arrays],
        in_specs=[pl.BlockSpec(memory_space=pl.ANY)] * (1 + len(arrays)),
        out_specs=[pl.BlockSpec(memory_space=pl.ANY)] * (1 + len(arrays)),
        scratch_shapes=[pltpu.SemaphoreType.DMA((near + len(arrays),))],
        compiler_params=pltpu.CompilerParams(vmem_limit_bytes=4 * 2**20),
        cost_estimate=pl.CostEstimate(flops=0, bytes_accessed=size, transcendentals=0),
        name="preload",
    )(*(pltpu.with_memory_space_constraint(a, pltpu.HBM) for a in (halves, *arrays)))


def pair_add_kernel(kept, swapped, total, *, turn):
    rows = 8
    count = total.shape[0]

    def add(source, size, target):
        at = pl.ds(source, size)
        both = kept[at].astype(jnp.float32) + swapped[at].astype(jnp.float32)
        total[pl.ds(target, size)] = both.astype(total.dtype)

    @pl.loop(0, count - rows, step=rows)
    def _(i):
        add(i, rows, i + turn)

    add(count - rows, rows - turn, count - rows + turn)
    add(count - turn, turn, 0)


def pair_add(kept, swapped, turn):
    return pl.pallas_call(
        functools.partial(pair_add_kernel, turn=turn),
        out_shape=pltpu.VMEM(kept.shape, kept.dtype),
        in_specs=[pl.BlockSpec(memory_space=pltpu.VMEM)] * 2,
        out_specs=pl.BlockSpec(memory_space=pltpu.VMEM),
        compiler_params=pltpu.CompilerParams(vmem_limit_bytes=8 * 2**20),
        name="pair_add",
    )(kept, pltpu.with_memory_space_constraint(swapped, pltpu.VMEM))


def pair_sums(arrived, j):
    count, _, share, width = arrived.shape
    half = count // 2
    size = half * share
    first = arrived[1 : half + 1, j].reshape(size, width)
    most = arrived[half + 1 :, j].reshape(size - share, width)
    other = jnp.concatenate([most, arrived[0, j]], axis=0)
    return first, other


def direction_kernel(arrived, root_left, root_right, moment, second, step, held, sem):
    owned = root_left.shape[0]
    ranks = held.shape[1]
    cuts = sem.shape[1] - 1
    copies = []
    for j in range(owned):
        first, other = pair_sums(arrived, j)
        left = root_left[j]
        right = root_right[j]
        left_high, left_low = split_half(dot(left, first) + dot(left, other))
        gradient = first.astype(jnp.float32) + other.astype(jnp.float32)
        moment_new = moment_decay * moment[j] + (1.0 - moment_decay) * gradient
        second_new = square_decay * second[j] + (1.0 - square_decay) * gradient * gradient
        divisor = second_new * lax.rsqrt(second_new) + adam_epsilon
        adam_dir = moment_new * lax.rsqrt(divisor * divisor)
        adam_sum = jnp.sum(adam_dir * adam_dir)
        conditioned = dot(left_high, right) + dot(left_low, right)
        cond_sum = jnp.sum(conditioned * conditioned)
        graft = jnp.sqrt(adam_sum) / (jnp.sqrt(cond_sum) + norm_epsilon)
        held[j] = (conditioned * graft).astype(jnp.bfloat16).reshape(held.shape[1:])
        edges = [c * (ranks // cuts) for c in range(cuts)] + [ranks - 1, ranks]
        for c in range(cuts + 1):
            start, size = edges[c], edges[c + 1] - edges[c]
            target = (start + 1) % ranks
            copy = pltpu.make_async_copy(
                held.at[j, pl.ds(start, size)], step.at[pl.ds(target, size), j], sem.at[j, c]
            )
            copy.start()
            copies.append(copy)
    for copy in copies:
        copy.wait()


def direction(arrived, root_left, root_right, moment, second):
    count, owned, share, width = arrived.shape
    ranks = count // 2
    return pl.pallas_call(
        direction_kernel,
        out_shape=pltpu.HBM((ranks, owned, share, width), jnp.bfloat16),
        in_specs=[pl.BlockSpec(memory_space=pltpu.VMEM)] * 5,
        out_specs=pl.BlockSpec(memory_space=pl.ANY),
        scratch_shapes=[
            pltpu.VMEM((owned, ranks, share, width), jnp.bfloat16),
            pltpu.SemaphoreType.DMA((owned, 5)),
        ],
        compiler_params=pltpu.CompilerParams(vmem_limit_bytes=24 * 2**20),
        cost_estimate=pl.CostEstimate(
            flops=owned * 8 * width**3, bytes_accessed=11 * 2**20, transcendentals=0
        ),
        name="direction",
    )(arrived, root_left, root_right, moment, second)


def gram(high, low, contract):
    def product(a, b):
        return lax.dot_general(
            a, b, (((contract,), (contract,)), ((), ())), preferred_element_type=jnp.float32
        )

    return product(high, high) + product(high, low) + product(low, high)


def statistics_kernel(
    arrived, stats_left, stats_right, moment, second, left_new, right_new, moment_new, second_new
):
    first, other = pair_sums(arrived, 0)
    gradient = first.astype(jnp.float32) + other.astype(jnp.float32)
    moment_new[0] = moment_decay * moment[0] + (1.0 - moment_decay) * gradient
    second_new[0] = square_decay * second[0] + (1.0 - square_decay) * gradient * gradient
    high, low = split_half(gradient)
    left_new[0] = stat_decay * stats_left[0] + (1.0 - stat_decay) * gram(high, low, 1)
    right_new[0] = stat_decay * stats_right[0] + (1.0 - stat_decay) * gram(high, low, 0)


def statistics(arrived, stats_left, stats_right, moment, second):
    count, owned, share, width = arrived.shape
    square = pl.BlockSpec((1, width, width), lambda j: (j, 0, 0))
    fixed = [pltpu.with_memory_space_constraint(a, pltpu.HBM) for a in (stats_left, stats_right, moment, second)]
    return pl.pallas_call(
        statistics_kernel,
        grid=(owned,),
        out_shape=[jax.ShapeDtypeStruct(stats_left.shape, jnp.float32)] * 4,
        in_specs=[pl.BlockSpec((count, 1, share, width), lambda j: (0, j, 0, 0))] + [square] * 4,
        out_specs=[square] * 4,
        compiler_params=pltpu.CompilerParams(vmem_limit_bytes=40 * 2**20),
        cost_estimate=pl.CostEstimate(
            flops=owned * 12 * width**3, bytes_accessed=18 * 2**20, transcendentals=0
        ),
        name="statistics",
    )(arrived, *fixed)


def widen_kernel(narrow, wide, held, sem):
    ranks = narrow.shape[0]
    cuts = sem.shape[0]
    size = ranks // cuts
    copies = []
    for c in range(cuts):
        at = pl.ds(c * size, size)
        if c < cuts - 1:
            held[at] = narrow[pl.ds(c * size + 1, size)].astype(jnp.float32)
        else:
            held[pl.ds(c * size, size - 1)] = narrow[pl.ds(c * size + 1, size - 1)].astype(jnp.float32)
            held[ranks - 1] = narrow[0].astype(jnp.float32)
        copy = pltpu.make_async_copy(held.at[at], wide.at[at], sem.at[c])
        copy.start()
        copies.append(copy)
    for copy in copies:
        copy.wait()


def widen(narrow):
    return pl.pallas_call(
        widen_kernel,
        out_shape=pltpu.HBM(narrow.shape, jnp.float32),
        in_specs=[pl.BlockSpec(memory_space=pltpu.VMEM)],
        out_specs=pl.BlockSpec(memory_space=pl.ANY),
        scratch_shapes=[
            pltpu.VMEM(narrow.shape, jnp.float32),
            pltpu.SemaphoreType.DMA((4,)),
        ],
        compiler_params=pltpu.CompilerParams(vmem_limit_bytes=8 * 2**20),
        name="widen",
    )(narrow)


def last_first(ranks):
    return ranks[-1:] + ranks[:-1]


def exchange(chunks, groups):
    return lax.all_to_all(
        chunks, every_axis, split_axis=0, concat_axis=0, tiled=True, axis_index_groups=groups
    )


def per_device(partials, stats_left, stats_right, root_left, root_right, moment, second):
    owned_count = stats_left.shape[0]
    fsdp_count = lax.axis_size("fsdp")
    near_count = lax.axis_size("near")
    pieces = partials[0]
    _, row_share, block_width = pieces.shape
    block = (row_share, block_width)
    halves = pieces.reshape(near_count, 2, fsdp_count * owned_count, *block)
    swapped = lax.ppermute(pick(halves), "core", [(0, 1), (1, 0)])
    kept, left_here, right_here, moment_here, second_here = preload(
        halves, root_left, root_right, moment, second
    )
    pair_sum = pair_add(kept.reshape(-1, *block), swapped.reshape(-1, *block), owned_count)

    def rank(near, core, fsdp):
        return (near * 2 + core) * fsdp_count + fsdp

    gather_groups = [
        last_first([rank(near, core, f) for near in range(near_count) for f in range(fsdp_count)])
        for core in range(2)
    ]
    return_groups = [
        last_first([rank(near, core, f) for f in range(fsdp_count)])
        for near in range(near_count)
        for core in range(2)
    ]
    arrived = exchange(pair_sum.reshape(-1, owned_count, *block), gather_groups)
    step = direction(arrived, left_here, right_here, moment_here, second_here)
    returned = exchange(step, return_groups)
    step_out = widen(returned).reshape(-1, *block)
    news = statistics(arrived, stats_left, stats_right, moment, second)
    return (*news, step_out)


def solution(mesh):
    fine = Mesh(mesh.devices.reshape(2, 2, -1), every_axis)
    owned = P(every_axis, None, None)
    return jax.shard_map(
        per_device,
        mesh=fine,
        in_specs=(P(("near", "core"), None, "fsdp", None), owned, owned, owned, owned, owned, owned),
        out_specs=(owned, owned, owned, owned, P(("near", "core"), "fsdp", None)),
        check_vma=False,
    )
```

```python
import functools

import jax
import jax.numpy as jnp
from jax import lax
from jax.experimental import pallas as pl
from jax.experimental.pallas import tpu as pltpu
from jax.sharding import Mesh, PartitionSpec as P

stat_decay = 0.95
moment_decay = 0.9
square_decay = 0.95
adam_epsilon = 1e-08
norm_epsilon = 1e-06
every_axis = ("near", "core", "fsdp")


def split_half(values):
    high = values.astype(jnp.bfloat16)
    low = (values - high.astype(jnp.float32)).astype(jnp.bfloat16)
    return high, low


def dot(a, b):
    return jnp.dot(a, b, preferred_element_type=jnp.float32)


def pick_kernel(halves, outgoing, sem):
    core = lax.axis_index("core")
    near, cuts = sem.shape
    count = halves.shape[2] // cuts
    copies = []
    for n in range(near):
        for c in range(cuts):
            at = pl.ds(c * count, count)
            copies.append(
                pltpu.make_async_copy(halves.at[n, 1 - core, at], outgoing.at[n, at], sem.at[n, c])
            )
    for copy in copies:
        copy.start()
    for copy in copies:
        copy.wait()


def pick(halves):
    near, _, *rest = halves.shape
    return pl.pallas_call(
        pick_kernel,
        out_shape=jax.ShapeDtypeStruct((near, *rest), halves.dtype),
        in_specs=[pl.BlockSpec(memory_space=pl.ANY)],
        out_specs=pl.BlockSpec(memory_space=pl.ANY),
        scratch_shapes=[pltpu.SemaphoreType.DMA((near, 4))],
        compiler_params=pltpu.CompilerParams(vmem_limit_bytes=4 * 2**20),
        name="pick",
    )(pltpu.with_memory_space_constraint(halves, pltpu.HBM))


def preload_kernel(halves, *refs):
    count = (len(refs) - 1) // 2
    sources, targets, sem = refs[:count], refs[count : 2 * count + 1], refs[-1]
    core = lax.axis_index("core")
    near = halves.shape[0]
    copies = [
        pltpu.make_async_copy(halves.at[n, core], targets[0].at[n], sem.at[n]) for n in range(near)
    ]
    for n, (source, target) in enumerate(zip(sources, targets[1:])):
        copies.append(pltpu.make_async_copy(source, target, sem.at[near + n]))
    for copy in copies:
        copy.start()
    for copy in copies:
        copy.wait()


def preload(halves, *arrays):
    near, _, *rest = halves.shape
    size = sum(a.size * a.dtype.itemsize for a in (halves, *arrays))
    return pl.pallas_call(
        preload_kernel,
        out_shape=[pltpu.VMEM((near, *rest), halves.dtype)]
        + [pltpu.VMEM(a.shape, a.dtype) for a in arrays],
        in_specs=[pl.BlockSpec(memory_space=pl.ANY)] * (1 + len(arrays)),
        out_specs=[pl.BlockSpec(memory_space=pl.ANY)] * (1 + len(arrays)),
        scratch_shapes=[pltpu.SemaphoreType.DMA((near + len(arrays),))],
        compiler_params=pltpu.CompilerParams(vmem_limit_bytes=4 * 2**20),
        cost_estimate=pl.CostEstimate(flops=0, bytes_accessed=size, transcendentals=0),
        name="preload",
    )(*(pltpu.with_memory_space_constraint(a, pltpu.HBM) for a in (halves, *arrays)))


def pair_add_kernel(kept, swapped, total, *, turn):
    rows = 8
    count = total.shape[0]

    def add(source, size, target):
        at = pl.ds(source, size)
        both = kept[at].astype(jnp.float32) + swapped[at].astype(jnp.float32)
        total[pl.ds(target, size)] = both.astype(total.dtype)

    @pl.loop(0, count - rows, step=rows)
    def _(i):
        add(i, rows, i + turn)

    add(count - rows, rows - turn, count - rows + turn)
    add(count - turn, turn, 0)


def pair_add(kept, swapped, turn):
    return pl.pallas_call(
        functools.partial(pair_add_kernel, turn=turn),
        out_shape=pltpu.VMEM(kept.shape, kept.dtype),
        in_specs=[pl.BlockSpec(memory_space=pltpu.VMEM)] * 2,
        out_specs=pl.BlockSpec(memory_space=pltpu.VMEM),
        compiler_params=pltpu.CompilerParams(vmem_limit_bytes=8 * 2**20),
        name="pair_add",
    )(kept, pltpu.with_memory_space_constraint(swapped, pltpu.VMEM))


def pair_sums(arrived, j):
    count, _, share, width = arrived.shape
    half = count // 2
    size = half * share
    first = arrived[1 : half + 1, j].reshape(size, width)
    most = arrived[half + 1 :, j].reshape(size - share, width)
    other = jnp.concatenate([most, arrived[0, j]], axis=0)
    return first, other


def direction_kernel(arrived, root_left, root_right, moment, second, step, held, sem):
    owned = root_left.shape[0]
    ranks = held.shape[1]
    cuts = sem.shape[1] - 1
    width = root_left.shape[-1]
    half, quarter = width // 2, width // 4
    copies = []
    for j in range(owned):
        first, other = pair_sums(arrived, j)

        def adam_squares(part):
            at = slice(part * quarter, (part + 1) * quarter)
            gradient = first[at].astype(jnp.float32) + other[at].astype(jnp.float32)
            moment_new = moment_decay * moment[j, at] + (1.0 - moment_decay) * gradient
            second_new = square_decay * second[j, at] + (1.0 - square_decay) * gradient * gradient
            divisor = second_new * lax.rsqrt(second_new) + adam_epsilon
            adam_dir = moment_new * lax.rsqrt(divisor * divisor)
            return jnp.sum((adam_dir * adam_dir).reshape(quarter // 8, 8, width), axis=0)

        left = root_left[j]
        right = root_right[j]
        applied, conditioned, squares = [], [], []
        for n in range(2):
            at = slice(n * half, (n + 1) * half)
            gradient = first[:, at].astype(jnp.float32) + other[:, at].astype(jnp.float32)
            applied.append(dot(left, gradient.astype(jnp.bfloat16)))
            squares.append(adam_squares(n))
        left_applied = jnp.concatenate(applied, axis=1).astype(jnp.bfloat16)
        for n in range(2):
            at = slice(n * half, (n + 1) * half)
            conditioned.append(dot(left_applied, right[:, at]))
            squares.append(adam_squares(2 + n))
        conditioned = jnp.concatenate(conditioned, axis=1)
        adam_sum = jnp.sum(squares[0] + squares[1] + squares[2] + squares[3])
        cond_sum = jnp.sum(conditioned * conditioned)
        graft = jnp.sqrt(adam_sum) / (jnp.sqrt(cond_sum) + norm_epsilon)
        held[j] = (conditioned * graft).astype(jnp.bfloat16).reshape(held.shape[1:])
        edges = [c * (ranks // cuts) for c in range(cuts)] + [ranks - 1, ranks]
        for c in range(cuts + 1):
            start, size = edges[c], edges[c + 1] - edges[c]
            target = (start + 1) % ranks
            copy = pltpu.make_async_copy(
                held.at[j, pl.ds(start, size)], step.at[pl.ds(target, size), j], sem.at[j, c]
            )
            copy.start()
            copies.append(copy)
    for copy in copies:
        copy.wait()


def direction(arrived, root_left, root_right, moment, second):
    count, owned, share, width = arrived.shape
    ranks = count // 2
    return pl.pallas_call(
        direction_kernel,
        out_shape=pltpu.HBM((ranks, owned, share, width), jnp.bfloat16),
        in_specs=[pl.BlockSpec(memory_space=pltpu.VMEM)] * 5,
        out_specs=pl.BlockSpec(memory_space=pl.ANY),
        scratch_shapes=[
            pltpu.VMEM((owned, ranks, share, width), jnp.bfloat16),
            pltpu.SemaphoreType.DMA((owned, 5)),
        ],
        compiler_params=pltpu.CompilerParams(vmem_limit_bytes=24 * 2**20),
        cost_estimate=pl.CostEstimate(
            flops=owned * 4 * width**3, bytes_accessed=11 * 2**20, transcendentals=0
        ),
        name="direction",
    )(arrived, root_left, root_right, moment, second)


def gram(high, low, contract):
    def product(a, b):
        return lax.dot_general(
            a, b, (((contract,), (contract,)), ((), ())), preferred_element_type=jnp.float32
        )

    return product(high, high) + product(high, low) + product(low, high)


def statistics_kernel(
    arrived, stats_left, stats_right, moment, second, left_new, right_new, moment_new, second_new
):
    first, other = pair_sums(arrived, 0)
    gradient = first.astype(jnp.float32) + other.astype(jnp.float32)
    moment_new[0] = moment_decay * moment[0] + (1.0 - moment_decay) * gradient
    second_new[0] = square_decay * second[0] + (1.0 - square_decay) * gradient * gradient
    high, low = split_half(gradient)
    left_new[0] = stat_decay * stats_left[0] + (1.0 - stat_decay) * gram(high, low, 1)
    right_new[0] = stat_decay * stats_right[0] + (1.0 - stat_decay) * gram(high, low, 0)


def statistics(arrived, stats_left, stats_right, moment, second):
    count, owned, share, width = arrived.shape
    square = pl.BlockSpec((1, width, width), lambda j: (j, 0, 0))
    fixed = [pltpu.with_memory_space_constraint(a, pltpu.HBM) for a in (stats_left, stats_right, moment, second)]
    return pl.pallas_call(
        statistics_kernel,
        grid=(owned,),
        out_shape=[jax.ShapeDtypeStruct(stats_left.shape, jnp.float32)] * 4,
        in_specs=[pl.BlockSpec((count, 1, share, width), lambda j: (0, j, 0, 0))] + [square] * 4,
        out_specs=[square] * 4,
        compiler_params=pltpu.CompilerParams(vmem_limit_bytes=40 * 2**20),
        cost_estimate=pl.CostEstimate(
            flops=owned * 12 * width**3, bytes_accessed=18 * 2**20, transcendentals=0
        ),
        name="statistics",
    )(arrived, *fixed)


def widen_kernel(narrow, wide, held, sem):
    ranks = narrow.shape[0]
    cuts = sem.shape[0]
    size = ranks // cuts
    copies = []
    for c in range(cuts):
        at = pl.ds(c * size, size)
        if c < cuts - 1:
            held[at] = narrow[pl.ds(c * size + 1, size)].astype(jnp.float32)
        else:
            held[pl.ds(c * size, size - 1)] = narrow[pl.ds(c * size + 1, size - 1)].astype(jnp.float32)
            held[ranks - 1] = narrow[0].astype(jnp.float32)
        copy = pltpu.make_async_copy(held.at[at], wide.at[at], sem.at[c])
        copy.start()
        copies.append(copy)
    for copy in copies:
        copy.wait()


def widen(narrow):
    return pl.pallas_call(
        widen_kernel,
        out_shape=pltpu.HBM(narrow.shape, jnp.float32),
        in_specs=[pl.BlockSpec(memory_space=pltpu.VMEM)],
        out_specs=pl.BlockSpec(memory_space=pl.ANY),
        scratch_shapes=[
            pltpu.VMEM(narrow.shape, jnp.float32),
            pltpu.SemaphoreType.DMA((4,)),
        ],
        compiler_params=pltpu.CompilerParams(vmem_limit_bytes=8 * 2**20),
        name="widen",
    )(narrow)


def last_first(ranks):
    return ranks[-1:] + ranks[:-1]


def exchange(chunks, groups):
    return lax.all_to_all(
        chunks, every_axis, split_axis=0, concat_axis=0, tiled=True, axis_index_groups=groups
    )


def per_device(partials, stats_left, stats_right, root_left, root_right, moment, second):
    owned_count = stats_left.shape[0]
    fsdp_count = lax.axis_size("fsdp")
    near_count = lax.axis_size("near")
    pieces = partials[0]
    _, row_share, block_width = pieces.shape
    block = (row_share, block_width)
    halves = pieces.reshape(near_count, 2, fsdp_count * owned_count, *block)
    swapped = lax.ppermute(pick(halves), "core", [(0, 1), (1, 0)])
    kept, left_here, right_here, moment_here, second_here = preload(
        halves, root_left, root_right, moment, second
    )
    pair_sum = pair_add(kept.reshape(-1, *block), swapped.reshape(-1, *block), owned_count)

    def rank(near, core, fsdp):
        return (near * 2 + core) * fsdp_count + fsdp

    gather_groups = [
        last_first([rank(near, core, f) for near in range(near_count) for f in range(fsdp_count)])
        for core in range(2)
    ]
    return_groups = [
        last_first([rank(near, core, f) for f in range(fsdp_count)])
        for near in range(near_count)
        for core in range(2)
    ]
    arrived = exchange(pair_sum.reshape(-1, owned_count, *block), gather_groups)
    step = direction(arrived, left_here, right_here, moment_here, second_here)
    returned = exchange(step, return_groups)
    step_out = widen(returned).reshape(-1, *block)
    news = statistics(arrived, stats_left, stats_right, moment, second)
    return (*news, step_out)


def solution(mesh):
    fine = Mesh(mesh.devices.reshape(2, 2, -1), every_axis)
    owned = P(every_axis, None, None)
    return jax.shard_map(
        per_device,
        mesh=fine,
        in_specs=(P(("near", "core"), None, "fsdp", None), owned, owned, owned, owned, owned, owned),
        out_specs=(owned, owned, owned, owned, P(("near", "core"), "fsdp", None)),
        check_vma=False,
    )
```

```python
import functools

import jax
import jax.numpy as jnp
from jax import lax
from jax.experimental import pallas as pl
from jax.experimental.pallas import tpu as pltpu
from jax.sharding import Mesh, PartitionSpec as P

stat_decay = 0.95
moment_decay = 0.9
square_decay = 0.95
adam_epsilon = 1e-08
norm_epsilon = 1e-06
every_axis = ("near", "core", "fsdp")


def split_half(values):
    high = values.astype(jnp.bfloat16)
    low = (values - high.astype(jnp.float32)).astype(jnp.bfloat16)
    return high, low


def dot(a, b):
    return jnp.dot(a, b, preferred_element_type=jnp.float32)


def pick_kernel(halves, *refs):
    *outgoing, sem = refs
    core = lax.axis_index("core")
    copies = [
        pltpu.make_async_copy(halves.at[n, 1 - core], target, sem.at[n])
        for n, target in enumerate(outgoing)
    ]
    for copy in copies:
        copy.start()
    for copy in copies:
        copy.wait()


def pick(halves):
    near, _, *rest = halves.shape
    return pl.pallas_call(
        pick_kernel,
        out_shape=[jax.ShapeDtypeStruct(rest, halves.dtype)] * near,
        in_specs=[pl.BlockSpec(memory_space=pl.ANY)],
        out_specs=[pl.BlockSpec(memory_space=pl.ANY)] * near,
        scratch_shapes=[pltpu.SemaphoreType.DMA((near,))],
        compiler_params=pltpu.CompilerParams(vmem_limit_bytes=4 * 2**20),
        name="pick",
    )(pltpu.with_memory_space_constraint(halves, pltpu.HBM))


def preload_kernel(halves, *refs):
    count = (len(refs) - 1) // 2
    sources, targets, sem = refs[:count], refs[count : 2 * count + 1], refs[-1]
    core = lax.axis_index("core")
    near = halves.shape[0]
    copies = [
        pltpu.make_async_copy(halves.at[n, core], targets[0].at[n], sem.at[n]) for n in range(near)
    ]
    for n, (source, target) in enumerate(zip(sources, targets[1:])):
        copies.append(pltpu.make_async_copy(source, target, sem.at[near + n]))
    for copy in copies:
        copy.start()
    for copy in copies:
        copy.wait()


def preload(halves, *arrays):
    near, _, *rest = halves.shape
    size = sum(a.size * a.dtype.itemsize for a in (halves, *arrays))
    return pl.pallas_call(
        preload_kernel,
        out_shape=[pltpu.VMEM((near, *rest), halves.dtype)]
        + [pltpu.VMEM(a.shape, a.dtype) for a in arrays],
        in_specs=[pl.BlockSpec(memory_space=pl.ANY)] * (1 + len(arrays)),
        out_specs=[pl.BlockSpec(memory_space=pl.ANY)] * (1 + len(arrays)),
        scratch_shapes=[pltpu.SemaphoreType.DMA((near + len(arrays),))],
        compiler_params=pltpu.CompilerParams(vmem_limit_bytes=4 * 2**20),
        cost_estimate=pl.CostEstimate(flops=0, bytes_accessed=size, transcendentals=0),
        name="preload",
    )(*(pltpu.with_memory_space_constraint(a, pltpu.HBM) for a in (halves, *arrays)))


def pair_add_kernel(kept, *refs, turn):
    *swapped, total = refs
    rows = 8
    count = swapped[0].shape[0]
    last = len(swapped) - 1

    def add(n, source, size):
        both = kept[pl.ds(n * count + source, size)].astype(jnp.float32)
        both = both + swapped[n][pl.ds(source, size)].astype(jnp.float32)
        total[pl.ds(n * count + source + turn, size)] = both.astype(total.dtype)

    for n in range(last + 1):
        pl.loop(0, count - rows if n == last else count, step=rows)(
            lambda i, n=n: add(n, i, rows)
        )
    add(last, count - rows, rows - turn)
    ends = count - turn
    both = kept[last * count + ends :].astype(jnp.float32)
    both = both + swapped[last][ends:].astype(jnp.float32)
    total[:turn] = both.astype(total.dtype)


def pair_add(kept, swapped, turn):
    inputs = [kept] + [pltpu.with_memory_space_constraint(a, pltpu.VMEM) for a in swapped]
    return pl.pallas_call(
        functools.partial(pair_add_kernel, turn=turn),
        out_shape=pltpu.VMEM(kept.shape, kept.dtype),
        in_specs=[pl.BlockSpec(memory_space=pltpu.VMEM)] * len(inputs),
        out_specs=pl.BlockSpec(memory_space=pltpu.VMEM),
        compiler_params=pltpu.CompilerParams(vmem_limit_bytes=8 * 2**20),
        name="pair_add",
    )(*inputs)


def pair_sums(arrived, j):
    count, _, share, width = arrived.shape
    half = count // 2
    size = half * share
    first = arrived[1 : half + 1, j].reshape(size, width)
    most = arrived[half + 1 :, j].reshape(size - share, width)
    other = jnp.concatenate([most, arrived[0, j]], axis=0)
    return first, other


def direction_kernel(arrived, root_left, root_right, moment, second, step, held, sem):
    owned = root_left.shape[0]
    ranks = held.shape[1]
    cuts = sem.shape[1] - 1
    width = root_left.shape[-1]
    half, quarter = width // 2, width // 4
    copies = []
    for j in range(owned):
        first, other = pair_sums(arrived, j)

        def adam_squares(part):
            at = slice(part * quarter, (part + 1) * quarter)
            gradient = first[at].astype(jnp.float32) + other[at].astype(jnp.float32)
            moment_new = moment_decay * moment[j, at] + (1.0 - moment_decay) * gradient
            second_new = square_decay * second[j, at] + (1.0 - square_decay) * gradient * gradient
            divisor = second_new * lax.rsqrt(second_new) + adam_epsilon
            adam_dir = moment_new * lax.rsqrt(divisor * divisor)
            return jnp.sum((adam_dir * adam_dir).reshape(quarter // 8, 8, width), axis=0)

        left = root_left[j]
        right = root_right[j]
        applied, conditioned, squares = [], [], []
        for n in range(2):
            at = slice(n * half, (n + 1) * half)
            gradient = first[:, at].astype(jnp.float32) + other[:, at].astype(jnp.float32)
            applied.append(dot(left, gradient.astype(jnp.bfloat16)))
            squares.append(adam_squares(n))
        left_applied = jnp.concatenate(applied, axis=1).astype(jnp.bfloat16)
        for n in range(2):
            at = slice(n * half, (n + 1) * half)
            conditioned.append(dot(left_applied, right[:, at]))
            squares.append(adam_squares(2 + n))
        conditioned = jnp.concatenate(conditioned, axis=1)
        adam_sum = jnp.sum(squares[0] + squares[1] + squares[2] + squares[3])
        cond_sum = jnp.sum(conditioned * conditioned)
        graft = jnp.sqrt(adam_sum) / (jnp.sqrt(cond_sum) + norm_epsilon)
        held[j] = (conditioned * graft).astype(jnp.bfloat16).reshape(held.shape[1:])
        edges = [c * (ranks // cuts) for c in range(cuts)] + [ranks - 1, ranks]
        for c in range(cuts + 1):
            start, size = edges[c], edges[c + 1] - edges[c]
            target = (start + 1) % ranks
            copy = pltpu.make_async_copy(
                held.at[j, pl.ds(start, size)], step.at[pl.ds(target, size), j], sem.at[j, c]
            )
            copy.start()
            copies.append(copy)
    for copy in copies:
        copy.wait()


def direction(arrived, root_left, root_right, moment, second):
    count, owned, share, width = arrived.shape
    ranks = count // 2
    return pl.pallas_call(
        direction_kernel,
        out_shape=pltpu.HBM((ranks, owned, share, width), jnp.bfloat16),
        in_specs=[pl.BlockSpec(memory_space=pltpu.VMEM)] * 5,
        out_specs=pl.BlockSpec(memory_space=pl.ANY),
        scratch_shapes=[
            pltpu.VMEM((owned, ranks, share, width), jnp.bfloat16),
            pltpu.SemaphoreType.DMA((owned, 5)),
        ],
        compiler_params=pltpu.CompilerParams(vmem_limit_bytes=24 * 2**20),
        cost_estimate=pl.CostEstimate(
            flops=owned * 4 * width**3, bytes_accessed=11 * 2**20, transcendentals=0
        ),
        name="direction",
    )(arrived, root_left, root_right, moment, second)


def gram(high, low, contract):
    def product(a, b):
        return lax.dot_general(
            a, b, (((contract,), (contract,)), ((), ())), preferred_element_type=jnp.float32
        )

    return product(high, high) + product(high, low) + product(low, high)


def statistics_kernel(
    arrived, stats_left, stats_right, moment, second, left_new, right_new, moment_new, second_new
):
    first, other = pair_sums(arrived, 0)
    gradient = first.astype(jnp.float32) + other.astype(jnp.float32)
    moment_new[0] = moment_decay * moment[0] + (1.0 - moment_decay) * gradient
    second_new[0] = square_decay * second[0] + (1.0 - square_decay) * gradient * gradient
    high, low = split_half(gradient)
    left_new[0] = stat_decay * stats_left[0] + (1.0 - stat_decay) * gram(high, low, 1)
    right_new[0] = stat_decay * stats_right[0] + (1.0 - stat_decay) * gram(high, low, 0)


def statistics(arrived, stats_left, stats_right, moment, second):
    count, owned, share, width = arrived.shape
    square = pl.BlockSpec((1, width, width), lambda j: (j, 0, 0))
    fixed = [pltpu.with_memory_space_constraint(a, pltpu.HBM) for a in (stats_left, stats_right, moment, second)]
    return pl.pallas_call(
        statistics_kernel,
        grid=(owned,),
        out_shape=[jax.ShapeDtypeStruct(stats_left.shape, jnp.float32)] * 4,
        in_specs=[pl.BlockSpec((count, 1, share, width), lambda j: (0, j, 0, 0))] + [square] * 4,
        out_specs=[square] * 4,
        compiler_params=pltpu.CompilerParams(vmem_limit_bytes=40 * 2**20),
        cost_estimate=pl.CostEstimate(
            flops=owned * 12 * width**3, bytes_accessed=18 * 2**20, transcendentals=0
        ),
        name="statistics",
    )(arrived, *fixed)


def widen_kernel(narrow, wide, held, sem):
    ranks = narrow.shape[0]
    cuts = sem.shape[0]
    size = ranks // cuts
    copies = []
    for c in range(cuts):
        at = pl.ds(c * size, size)
        if c < cuts - 1:
            held[at] = narrow[pl.ds(c * size + 1, size)].astype(jnp.float32)
        else:
            held[pl.ds(c * size, size - 1)] = narrow[pl.ds(c * size + 1, size - 1)].astype(jnp.float32)
            held[ranks - 1] = narrow[0].astype(jnp.float32)
        copy = pltpu.make_async_copy(held.at[at], wide.at[at], sem.at[c])
        copy.start()
        copies.append(copy)
    for copy in copies:
        copy.wait()


def widen(narrow):
    return pl.pallas_call(
        widen_kernel,
        out_shape=pltpu.HBM(narrow.shape, jnp.float32),
        in_specs=[pl.BlockSpec(memory_space=pltpu.VMEM)],
        out_specs=pl.BlockSpec(memory_space=pl.ANY),
        scratch_shapes=[
            pltpu.VMEM(narrow.shape, jnp.float32),
            pltpu.SemaphoreType.DMA((4,)),
        ],
        compiler_params=pltpu.CompilerParams(vmem_limit_bytes=8 * 2**20),
        name="widen",
    )(narrow)


def last_first(ranks):
    return ranks[-1:] + ranks[:-1]


def exchange(chunks, groups):
    return lax.all_to_all(
        chunks, every_axis, split_axis=0, concat_axis=0, tiled=True, axis_index_groups=groups
    )


def per_device(partials, stats_left, stats_right, root_left, root_right, moment, second):
    owned_count = stats_left.shape[0]
    fsdp_count = lax.axis_size("fsdp")
    near_count = lax.axis_size("near")
    pieces = partials[0]
    _, row_share, block_width = pieces.shape
    block = (row_share, block_width)
    halves = pieces.reshape(near_count, 2, fsdp_count * owned_count, *block)
    swapped = [lax.ppermute(part, "core", [(0, 1), (1, 0)]) for part in pick(halves)]
    kept, left_here, right_here, moment_here, second_here = preload(
        halves, root_left, root_right, moment, second
    )
    pair_sum = pair_add(kept.reshape(-1, *block), swapped, owned_count)

    def rank(near, core, fsdp):
        return (near * 2 + core) * fsdp_count + fsdp

    gather_groups = [
        last_first([rank(near, core, f) for near in range(near_count) for f in range(fsdp_count)])
        for core in range(2)
    ]
    return_groups = [
        last_first([rank(near, core, f) for f in range(fsdp_count)])
        for near in range(near_count)
        for core in range(2)
    ]
    arrived = exchange(pair_sum.reshape(-1, owned_count, *block), gather_groups)
    step = direction(arrived, left_here, right_here, moment_here, second_here)
    returned = exchange(step, return_groups)
    step_out = widen(returned).reshape(-1, *block)
    news = statistics(arrived, stats_left, stats_right, moment, second)
    return (*news, step_out)


def solution(mesh):
    fine = Mesh(mesh.devices.reshape(2, 2, -1), every_axis)
    owned = P(every_axis, None, None)
    return jax.shard_map(
        per_device,
        mesh=fine,
        in_specs=(P(("near", "core"), None, "fsdp", None), owned, owned, owned, owned, owned, owned),
        out_specs=(owned, owned, owned, owned, P(("near", "core"), "fsdp", None)),
        check_vma=False,
    )
```

```python
import functools

import jax
import jax.numpy as jnp
from jax import lax
from jax.experimental import pallas as pl
from jax.experimental.pallas import tpu as pltpu
from jax.sharding import Mesh, PartitionSpec as P

stat_decay = 0.95
moment_decay = 0.9
square_decay = 0.95
adam_epsilon = 1e-08
norm_epsilon = 1e-06
every_axis = ("near", "core", "fsdp")


def split_half(values):
    high = values.astype(jnp.bfloat16)
    low = (values - high.astype(jnp.float32)).astype(jnp.bfloat16)
    return high, low


def dot(a, b):
    return jnp.dot(a, b, preferred_element_type=jnp.float32)


def pick_kernel(halves, *refs):
    *outgoing, sem = refs
    core = lax.axis_index("core")
    copies = [
        pltpu.make_async_copy(halves.at[n, 1 - core], target, sem.at[n])
        for n, target in enumerate(outgoing)
    ]
    for copy in copies:
        copy.start()
    for copy in copies:
        copy.wait()


def pick(halves):
    near, _, *rest = halves.shape
    return pl.pallas_call(
        pick_kernel,
        out_shape=[jax.ShapeDtypeStruct(rest, halves.dtype)] * near,
        in_specs=[pl.BlockSpec(memory_space=pl.ANY)],
        out_specs=[pl.BlockSpec(memory_space=pl.ANY)] * near,
        scratch_shapes=[pltpu.SemaphoreType.DMA((near,))],
        compiler_params=pltpu.CompilerParams(vmem_limit_bytes=4 * 2**20),
        name="pick",
    )(pltpu.with_memory_space_constraint(halves, pltpu.HBM))


def preload_kernel(halves, *refs):
    count = (len(refs) - 1) // 2
    sources, targets, sem = refs[:count], refs[count : 2 * count + 1], refs[-1]
    core = lax.axis_index("core")
    near = halves.shape[0]
    copies = [
        pltpu.make_async_copy(halves.at[n, core], targets[0].at[n], sem.at[n]) for n in range(near)
    ]
    for n, (source, target) in enumerate(zip(sources, targets[1:])):
        copies.append(pltpu.make_async_copy(source, target, sem.at[near + n]))
    for copy in copies:
        copy.start()
    for copy in copies:
        copy.wait()


def preload(halves, *arrays):
    near, _, *rest = halves.shape
    size = sum(a.size * a.dtype.itemsize for a in (halves, *arrays))
    return pl.pallas_call(
        preload_kernel,
        out_shape=[pltpu.VMEM((near, *rest), halves.dtype)]
        + [pltpu.VMEM(a.shape, a.dtype) for a in arrays],
        in_specs=[pl.BlockSpec(memory_space=pl.ANY)] * (1 + len(arrays)),
        out_specs=[pl.BlockSpec(memory_space=pl.ANY)] * (1 + len(arrays)),
        scratch_shapes=[pltpu.SemaphoreType.DMA((near + len(arrays),))],
        compiler_params=pltpu.CompilerParams(vmem_limit_bytes=4 * 2**20),
        cost_estimate=pl.CostEstimate(flops=0, bytes_accessed=size, transcendentals=0),
        name="preload",
    )(*(pltpu.with_memory_space_constraint(a, pltpu.HBM) for a in (halves, *arrays)))


def pair_add_kernel(kept, *refs, turn):
    *swapped, total = refs
    rows = 8
    count = swapped[0].shape[0]
    last = len(swapped) - 1

    def add(n, source, size, target):
        both = kept[pl.ds(n * count + source, size)] + swapped[n][pl.ds(source, size)]
        total[pl.ds(target, size)] = both

    for n in range(last + 1):
        pl.loop(0, count - rows if n == last else count, step=rows, unroll=2 if n < last else 1)(
            lambda i, n=n: add(n, i, rows, n * count + i + turn)
        )
    add(last, count - rows, rows - turn, total.shape[0] - rows + turn)
    add(last, count - turn, turn, 0)


def pair_add(kept, swapped, turn):
    inputs = [kept] + [pltpu.with_memory_space_constraint(a, pltpu.VMEM) for a in swapped]
    return pl.pallas_call(
        functools.partial(pair_add_kernel, turn=turn),
        out_shape=pltpu.VMEM(kept.shape, kept.dtype),
        in_specs=[pl.BlockSpec(memory_space=pltpu.VMEM)] * len(inputs),
        out_specs=pl.BlockSpec(memory_space=pltpu.VMEM),
        compiler_params=pltpu.CompilerParams(vmem_limit_bytes=8 * 2**20),
        name="pair_add",
    )(*inputs)


def pair_sums(arrived, j):
    count, _, share, width = arrived.shape
    half = count // 2
    size = half * share
    first = arrived[1 : half + 1, j].reshape(size, width)
    most = arrived[half + 1 :, j].reshape(size - share, width)
    other = jnp.concatenate([most, arrived[0, j]], axis=0)
    return first, other


def direction_kernel(arrived, root_left, root_right, moment, second, step, held, sem):
    owned = root_left.shape[0]
    ranks = held.shape[1]
    cuts = sem.shape[1] - 1
    width = root_left.shape[-1]
    half, quarter = width // 2, width // 4
    copies = []
    for j in range(owned):
        first, other = pair_sums(arrived, j)

        def adam_squares(part):
            at = slice(part * quarter, (part + 1) * quarter)
            gradient = first[at].astype(jnp.float32) + other[at].astype(jnp.float32)
            moment_new = moment_decay * moment[j, at] + (1.0 - moment_decay) * gradient
            second_new = square_decay * second[j, at] + (1.0 - square_decay) * gradient * gradient
            divisor = second_new * lax.rsqrt(second_new) + adam_epsilon
            adam_dir = moment_new * lax.rsqrt(divisor * divisor)
            return jnp.sum((adam_dir * adam_dir).reshape(quarter // 8, 8, width), axis=0)

        left = root_left[j]
        right = root_right[j]
        applied, conditioned, squares = [], [], []
        for n in range(2):
            at = slice(n * half, (n + 1) * half)
            gradient = first[:, at].astype(jnp.float32) + other[:, at].astype(jnp.float32)
            applied.append(dot(left, gradient.astype(jnp.bfloat16)))
            squares.append(adam_squares(n))
        left_applied = jnp.concatenate(applied, axis=1).astype(jnp.bfloat16)
        for n in range(2):
            at = slice(n * half, (n + 1) * half)
            conditioned.append(dot(left_applied, right[:, at]))
            squares.append(adam_squares(2 + n))
        conditioned = jnp.concatenate(conditioned, axis=1)
        adam_sum = jnp.sum(squares[0] + squares[1] + squares[2] + squares[3])
        cond_sum = jnp.sum(conditioned * conditioned)
        graft = jnp.sqrt(adam_sum) / (jnp.sqrt(cond_sum) + norm_epsilon)
        held[j] = (conditioned * graft).astype(jnp.bfloat16).reshape(held.shape[1:])
        edges = [c * (ranks // cuts) for c in range(cuts)] + [ranks - 1, ranks]
        for c in range(cuts + 1):
            start, size = edges[c], edges[c + 1] - edges[c]
            target = (start + 1) % ranks
            copy = pltpu.make_async_copy(
                held.at[j, pl.ds(start, size)], step.at[pl.ds(target, size), j], sem.at[j, c]
            )
            copy.start()
            copies.append(copy)
    for copy in copies:
        copy.wait()


def direction(arrived, root_left, root_right, moment, second):
    count, owned, share, width = arrived.shape
    ranks = count // 2
    return pl.pallas_call(
        direction_kernel,
        out_shape=pltpu.HBM((ranks, owned, share, width), jnp.bfloat16),
        in_specs=[pl.BlockSpec(memory_space=pltpu.VMEM)] * 5,
        out_specs=pl.BlockSpec(memory_space=pl.ANY),
        scratch_shapes=[
            pltpu.VMEM((owned, ranks, share, width), jnp.bfloat16),
            pltpu.SemaphoreType.DMA((owned, 5)),
        ],
        compiler_params=pltpu.CompilerParams(vmem_limit_bytes=24 * 2**20),
        cost_estimate=pl.CostEstimate(
            flops=owned * 4 * width**3, bytes_accessed=11 * 2**20, transcendentals=0
        ),
        name="direction",
    )(arrived, root_left, root_right, moment, second)


def gram(high, low, contract):
    def product(a, b):
        return lax.dot_general(
            a, b, (((contract,), (contract,)), ((), ())), preferred_element_type=jnp.float32
        )

    return product(high, high) + product(high, low) + product(low, high)


def statistics_kernel(
    arrived, stats_left, stats_right, moment, second, left_new, right_new, moment_new, second_new
):
    first, other = pair_sums(arrived, 0)
    gradient = first.astype(jnp.float32) + other.astype(jnp.float32)
    moment_new[0] = moment_decay * moment[0] + (1.0 - moment_decay) * gradient
    second_new[0] = square_decay * second[0] + (1.0 - square_decay) * gradient * gradient
    high, low = split_half(gradient)
    left_new[0] = stat_decay * stats_left[0] + (1.0 - stat_decay) * gram(high, low, 1)
    right_new[0] = stat_decay * stats_right[0] + (1.0 - stat_decay) * gram(high, low, 0)


def statistics(arrived, stats_left, stats_right, moment, second):
    count, owned, share, width = arrived.shape
    square = pl.BlockSpec((1, width, width), lambda j: (j, 0, 0))
    fixed = [pltpu.with_memory_space_constraint(a, pltpu.HBM) for a in (stats_left, stats_right, moment, second)]
    return pl.pallas_call(
        statistics_kernel,
        grid=(owned,),
        out_shape=[jax.ShapeDtypeStruct(stats_left.shape, jnp.float32)] * 4,
        in_specs=[pl.BlockSpec((count, 1, share, width), lambda j: (0, j, 0, 0))] + [square] * 4,
        out_specs=[square] * 4,
        compiler_params=pltpu.CompilerParams(vmem_limit_bytes=40 * 2**20),
        cost_estimate=pl.CostEstimate(
            flops=owned * 12 * width**3, bytes_accessed=18 * 2**20, transcendentals=0
        ),
        name="statistics",
    )(arrived, *fixed)


def widen_kernel(narrow, wide, held, sem):
    ranks = narrow.shape[0]
    cuts = sem.shape[0]
    size = ranks // cuts
    copies = []
    for c in range(cuts):
        at = pl.ds(c * size, size)
        if c < cuts - 1:
            held[at] = narrow[pl.ds(c * size + 1, size)].astype(jnp.float32)
        else:
            held[pl.ds(c * size, size - 1)] = narrow[pl.ds(c * size + 1, size - 1)].astype(jnp.float32)
            held[ranks - 1] = narrow[0].astype(jnp.float32)
        copy = pltpu.make_async_copy(held.at[at], wide.at[at], sem.at[c])
        copy.start()
        copies.append(copy)
    for copy in copies:
        copy.wait()


def widen(narrow):
    return pl.pallas_call(
        widen_kernel,
        out_shape=pltpu.HBM(narrow.shape, jnp.float32),
        in_specs=[pl.BlockSpec(memory_space=pltpu.VMEM)],
        out_specs=pl.BlockSpec(memory_space=pl.ANY),
        scratch_shapes=[
            pltpu.VMEM(narrow.shape, jnp.float32),
            pltpu.SemaphoreType.DMA((4,)),
        ],
        compiler_params=pltpu.CompilerParams(vmem_limit_bytes=8 * 2**20),
        name="widen",
    )(narrow)


def last_first(ranks):
    return ranks[-1:] + ranks[:-1]


def exchange(chunks, groups):
    return lax.all_to_all(
        chunks, every_axis, split_axis=0, concat_axis=0, tiled=True, axis_index_groups=groups
    )


def per_device(partials, stats_left, stats_right, root_left, root_right, moment, second):
    owned_count = stats_left.shape[0]
    fsdp_count = lax.axis_size("fsdp")
    near_count = lax.axis_size("near")
    pieces = partials[0]
    _, row_share, block_width = pieces.shape
    block = (row_share, block_width)
    halves = pieces.reshape(near_count, 2, fsdp_count * owned_count, *block)
    swapped = [lax.ppermute(part, "core", [(0, 1), (1, 0)]) for part in pick(halves)]
    kept, left_here, right_here, moment_here, second_here = preload(
        halves, root_left, root_right, moment, second
    )
    pair_sum = pair_add(kept.reshape(-1, *block), swapped, owned_count)

    def rank(near, core, fsdp):
        return (near * 2 + core) * fsdp_count + fsdp

    gather_groups = [
        last_first([rank(near, core, f) for near in range(near_count) for f in range(fsdp_count)])
        for core in range(2)
    ]
    return_groups = [
        last_first([rank(near, core, f) for f in range(fsdp_count)])
        for near in range(near_count)
        for core in range(2)
    ]
    arrived = exchange(pair_sum.reshape(-1, owned_count, *block), gather_groups)
    step = direction(arrived, left_here, right_here, moment_here, second_here)
    returned = exchange(step, return_groups)
    step_out = widen(returned).reshape(-1, *block)
    news = statistics(arrived, stats_left, stats_right, moment, second)
    return (*news, step_out)


def solution(mesh):
    fine = Mesh(mesh.devices.reshape(2, 2, -1), every_axis)
    owned = P(every_axis, None, None)
    return jax.shard_map(
        per_device,
        mesh=fine,
        in_specs=(P(("near", "core"), None, "fsdp", None), owned, owned, owned, owned, owned, owned),
        out_specs=(owned, owned, owned, owned, P(("near", "core"), "fsdp", None)),
        check_vma=False,
    )
```

```python
import functools

import jax
import jax.numpy as jnp
from jax import lax
from jax.experimental import pallas as pl
from jax.experimental.pallas import tpu as pltpu
from jax.sharding import Mesh, PartitionSpec as P

stat_decay = 0.95
moment_decay = 0.9
square_decay = 0.95
adam_epsilon = 1e-08
norm_epsilon = 1e-06
every_axis = ("near", "core", "fsdp")


def split_half(values):
    high = values.astype(jnp.bfloat16)
    low = (values - high.astype(jnp.float32)).astype(jnp.bfloat16)
    return high, low


def dot(a, b):
    return jnp.dot(a, b, preferred_element_type=jnp.float32)


def pick_kernel(halves, *refs):
    *outgoing, sem = refs
    core = lax.axis_index("core")
    copies = [
        pltpu.make_async_copy(halves.at[n, 1 - core], target, sem.at[n])
        for n, target in enumerate(outgoing)
    ]
    for copy in copies:
        copy.start()
    for copy in copies:
        copy.wait()


def pick(halves):
    near, _, *rest = halves.shape
    return pl.pallas_call(
        pick_kernel,
        out_shape=[jax.ShapeDtypeStruct(rest, halves.dtype)] * near,
        in_specs=[pl.BlockSpec(memory_space=pl.ANY)],
        out_specs=[pl.BlockSpec(memory_space=pl.ANY)] * near,
        scratch_shapes=[pltpu.SemaphoreType.DMA((near,))],
        compiler_params=pltpu.CompilerParams(vmem_limit_bytes=4 * 2**20),
        name="pick",
    )(pltpu.with_memory_space_constraint(halves, pltpu.HBM))


def preload_kernel(halves, *refs):
    count = (len(refs) - 1) // 2
    sources, targets, sem = refs[:count], refs[count : 2 * count + 1], refs[-1]
    core = lax.axis_index("core")
    near = halves.shape[0]
    copies = [
        pltpu.make_async_copy(halves.at[n, core], targets[0].at[n], sem.at[n]) for n in range(near)
    ]
    for n, (source, target) in enumerate(zip(sources, targets[1:])):
        copies.append(pltpu.make_async_copy(source, target, sem.at[near + n]))
    for copy in copies:
        copy.start()
    for copy in copies:
        copy.wait()


def preload(halves, *arrays):
    near, _, *rest = halves.shape
    size = sum(a.size * a.dtype.itemsize for a in (halves, *arrays))
    return pl.pallas_call(
        preload_kernel,
        out_shape=[pltpu.VMEM((near, *rest), halves.dtype)]
        + [pltpu.VMEM(a.shape, a.dtype) for a in arrays],
        in_specs=[pl.BlockSpec(memory_space=pl.ANY)] * (1 + len(arrays)),
        out_specs=[pl.BlockSpec(memory_space=pl.ANY)] * (1 + len(arrays)),
        scratch_shapes=[pltpu.SemaphoreType.DMA((near + len(arrays),))],
        compiler_params=pltpu.CompilerParams(vmem_limit_bytes=4 * 2**20),
        cost_estimate=pl.CostEstimate(flops=0, bytes_accessed=size, transcendentals=0),
        name="preload",
    )(*(pltpu.with_memory_space_constraint(a, pltpu.HBM) for a in (halves, *arrays)))


def pair_add_kernel(kept, *refs, turn):
    *swapped, total = refs
    rows = 8
    count = swapped[0].shape[0]
    last = len(swapped) - 1

    def add(n, source, size, target):
        both = kept[pl.ds(n * count + source, size)] + swapped[n][pl.ds(source, size)]
        total[pl.ds(target, size)] = both

    for n in range(last + 1):
        pl.loop(0, count - rows if n == last else count, step=rows, unroll=2 if n < last else 1)(
            lambda i, n=n: add(n, i, rows, n * count + i + turn)
        )
    add(last, count - rows, rows - turn, total.shape[0] - rows + turn)
    add(last, count - turn, turn, 0)


def pair_add(kept, swapped, turn):
    inputs = [kept] + [pltpu.with_memory_space_constraint(a, pltpu.VMEM) for a in swapped]
    return pl.pallas_call(
        functools.partial(pair_add_kernel, turn=turn),
        out_shape=pltpu.VMEM(kept.shape, kept.dtype),
        in_specs=[pl.BlockSpec(memory_space=pltpu.VMEM)] * len(inputs),
        out_specs=pl.BlockSpec(memory_space=pltpu.VMEM),
        compiler_params=pltpu.CompilerParams(vmem_limit_bytes=8 * 2**20),
        name="pair_add",
    )(*inputs)


def pair_sums(arrived, j):
    count, _, share, width = arrived.shape
    half = count // 2
    size = half * share
    first = arrived[1 : half + 1, j].reshape(size, width)
    most = arrived[half + 1 :, j].reshape(size - share, width)
    other = jnp.concatenate([most, arrived[0, j]], axis=0)
    return first, other


def direction_kernel(arrived, root_left, root_right, moment, second, step, held, sem):
    owned = root_left.shape[0]
    ranks = held.shape[1]
    cuts = sem.shape[1]
    width = root_left.shape[-1]
    half, quarter = width // 2, width // 4
    copies = []
    for j in range(owned):
        first, other = pair_sums(arrived, j)

        def adam_squares(part):
            at = slice(part * quarter, (part + 1) * quarter)
            gradient = first[at].astype(jnp.float32) + other[at].astype(jnp.float32)
            moment_new = moment_decay * moment[j, at] + (1.0 - moment_decay) * gradient
            second_new = square_decay * second[j, at] + (1.0 - square_decay) * gradient * gradient
            divisor = second_new * lax.rsqrt(second_new) + adam_epsilon
            adam_dir = moment_new * lax.rsqrt(divisor * divisor)
            return jnp.sum((adam_dir * adam_dir).reshape(quarter // 8, 8, width), axis=0)

        left = root_left[j]
        right = root_right[j]
        applied, conditioned, squares = [], [], []
        for n in range(2):
            at = slice(n * half, (n + 1) * half)
            gradient = first[:, at].astype(jnp.float32) + other[:, at].astype(jnp.float32)
            applied.append(dot(left, gradient.astype(jnp.bfloat16)))
            squares.append(adam_squares(n))
        left_applied = jnp.concatenate(applied, axis=1).astype(jnp.bfloat16)
        for n in range(2):
            at = slice(n * half, (n + 1) * half)
            conditioned.append(dot(left_applied, right[:, at]))
            squares.append(adam_squares(2 + n))
        conditioned = jnp.concatenate(conditioned, axis=1)
        adam_sum = jnp.sum(squares[0] + squares[1] + squares[2] + squares[3])
        cond_sum = jnp.sum(conditioned * conditioned)
        graft = jnp.sqrt(adam_sum) / (jnp.sqrt(cond_sum) + norm_epsilon)
        scaled = (conditioned * graft).astype(jnp.bfloat16).reshape(held.shape[1:])
        for rank in range(ranks):
            held[j, ranks - 1 - rank] = scaled[rank]
        for c in range(cuts):
            at = pl.ds(c * (ranks // cuts), ranks // cuts)
            copy = pltpu.make_async_copy(held.at[j, at], step.at[at, j], sem.at[j, c])
            copy.start()
            copies.append(copy)
    for copy in copies:
        copy.wait()


def direction(arrived, root_left, root_right, moment, second):
    count, owned, share, width = arrived.shape
    ranks = count // 2
    return pl.pallas_call(
        direction_kernel,
        out_shape=pltpu.HBM((ranks, owned, share, width), jnp.bfloat16),
        in_specs=[pl.BlockSpec(memory_space=pltpu.VMEM)] * 5,
        out_specs=pl.BlockSpec(memory_space=pl.ANY),
        scratch_shapes=[
            pltpu.VMEM((owned, ranks, share, width), jnp.bfloat16),
            pltpu.SemaphoreType.DMA((owned, 4)),
        ],
        compiler_params=pltpu.CompilerParams(vmem_limit_bytes=24 * 2**20),
        cost_estimate=pl.CostEstimate(
            flops=owned * 4 * width**3, bytes_accessed=11 * 2**20, transcendentals=0
        ),
        name="direction",
    )(arrived, root_left, root_right, moment, second)


def gram(high, low, contract):
    def product(a, b):
        return lax.dot_general(
            a, b, (((contract,), (contract,)), ((), ())), preferred_element_type=jnp.float32
        )

    return product(high, high) + product(high, low) + product(low, high)


def statistics_kernel(
    arrived, stats_left, stats_right, moment, second, left_new, right_new, moment_new, second_new
):
    first, other = pair_sums(arrived, 0)
    gradient = first.astype(jnp.float32) + other.astype(jnp.float32)
    moment_new[0] = moment_decay * moment[0] + (1.0 - moment_decay) * gradient
    second_new[0] = square_decay * second[0] + (1.0 - square_decay) * gradient * gradient
    high, low = split_half(gradient)
    left_new[0] = stat_decay * stats_left[0] + (1.0 - stat_decay) * gram(high, low, 1)
    right_new[0] = stat_decay * stats_right[0] + (1.0 - stat_decay) * gram(high, low, 0)


def statistics(arrived, stats_left, stats_right, moment, second):
    count, owned, share, width = arrived.shape
    square = pl.BlockSpec((1, width, width), lambda j: (j, 0, 0))
    fixed = [pltpu.with_memory_space_constraint(a, pltpu.HBM) for a in (stats_left, stats_right, moment, second)]
    return pl.pallas_call(
        statistics_kernel,
        grid=(owned,),
        out_shape=[jax.ShapeDtypeStruct(stats_left.shape, jnp.float32)] * 4,
        in_specs=[pl.BlockSpec((count, 1, share, width), lambda j: (0, j, 0, 0))] + [square] * 4,
        out_specs=[square] * 4,
        compiler_params=pltpu.CompilerParams(vmem_limit_bytes=40 * 2**20),
        cost_estimate=pl.CostEstimate(
            flops=owned * 12 * width**3, bytes_accessed=18 * 2**20, transcendentals=0
        ),
        name="statistics",
    )(arrived, *fixed)


def widen_kernel(narrow, wide, held, sem):
    ranks = narrow.shape[0]
    cuts = sem.shape[0]
    size = ranks // cuts
    copies = []
    for c in range(cuts):
        at = pl.ds(c * size, size)
        for rank in range(c * size, (c + 1) * size):
            held[rank] = narrow[ranks - 1 - rank].astype(jnp.float32)
        copy = pltpu.make_async_copy(held.at[at], wide.at[at], sem.at[c])
        copy.start()
        copies.append(copy)
    for copy in copies:
        copy.wait()


def widen(narrow):
    return pl.pallas_call(
        widen_kernel,
        out_shape=pltpu.HBM(narrow.shape, jnp.float32),
        in_specs=[pl.BlockSpec(memory_space=pltpu.VMEM)],
        out_specs=pl.BlockSpec(memory_space=pl.ANY),
        scratch_shapes=[
            pltpu.VMEM(narrow.shape, jnp.float32),
            pltpu.SemaphoreType.DMA((4,)),
        ],
        compiler_params=pltpu.CompilerParams(vmem_limit_bytes=8 * 2**20),
        name="widen",
    )(narrow)


def last_first(ranks):
    return ranks[-1:] + ranks[:-1]


def exchange(chunks, groups):
    return lax.all_to_all(
        chunks, every_axis, split_axis=0, concat_axis=0, tiled=True, axis_index_groups=groups
    )


def per_device(partials, stats_left, stats_right, root_left, root_right, moment, second):
    owned_count = stats_left.shape[0]
    fsdp_count = lax.axis_size("fsdp")
    near_count = lax.axis_size("near")
    pieces = partials[0]
    _, row_share, block_width = pieces.shape
    block = (row_share, block_width)
    halves = pieces.reshape(near_count, 2, fsdp_count * owned_count, *block)
    swapped = [lax.ppermute(part, "core", [(0, 1), (1, 0)]) for part in pick(halves)]
    kept, left_here, right_here, moment_here, second_here = preload(
        halves, root_left, root_right, moment, second
    )
    pair_sum = pair_add(kept.reshape(-1, *block), swapped, owned_count)

    def rank(near, core, fsdp):
        return (near * 2 + core) * fsdp_count + fsdp

    gather_groups = [
        last_first([rank(near, core, f) for near in range(near_count) for f in range(fsdp_count)])
        for core in range(2)
    ]
    return_groups = [
        [rank(near, core, f) for f in reversed(range(fsdp_count))]
        for near in range(near_count)
        for core in range(2)
    ]
    arrived = exchange(pair_sum.reshape(-1, owned_count, *block), gather_groups)
    step = direction(arrived, left_here, right_here, moment_here, second_here)
    returned = exchange(step, return_groups)
    step_out = widen(returned).reshape(-1, *block)
    news = statistics(arrived, stats_left, stats_right, moment, second)
    return (*news, step_out)


def solution(mesh):
    fine = Mesh(mesh.devices.reshape(2, 2, -1), every_axis)
    owned = P(every_axis, None, None)
    return jax.shard_map(
        per_device,
        mesh=fine,
        in_specs=(P(("near", "core"), None, "fsdp", None), owned, owned, owned, owned, owned, owned),
        out_specs=(owned, owned, owned, owned, P(("near", "core"), "fsdp", None)),
        check_vma=False,
    )
```
